512 devices in a mesh: engine: 4 (over x), fsdp: 16 (over z, y_lo), tensor: 8 (over y_hi, core).
Axes of the slice: x: 4, y: 8 (y_hi: 4, y_lo: 2; y = y_hi * 2 + y_lo), z: 8, core: 2. Of those that a mesh axis runs over, the one named last changes fastest.
Arguments:
- layer_input: bfloat16 [8192, 16384], P(('engine', 'fsdp'), 'tensor'), may hold values from -6 to 6
- norm_gain: bfloat16 [16384], P('tensor'), may hold values from 0.099609375 to 1.8984375
- query_base: bfloat16 [16384, 1024], P(('engine', 'fsdp'), 'tensor'), may hold values from -0.046875 to 0.046875
- query_down: bfloat16 [16384, 64], P(('engine', 'fsdp')), may hold values from -0.046875 to 0.046875
- query_up: bfloat16 [64, 1024], P(None, 'tensor'), may hold values from -0.29882812 to 0.29882812
- kv_base: bfloat16 [8, 2048, 256], P('tensor', ('engine', 'fsdp')), may hold values from -0.046875 to 0.046875
- output_base_weight: bfloat16 [1024, 8, 2048], P(None, 'tensor', ('engine', 'fsdp')), may hold values from -0.1875 to 0.1875
- output_down_factor: bfloat16 [1024, 64], P('tensor'), may hold values from -0.1875 to 0.1875
- output_up_factor: bfloat16 [64, 8, 2048], P(None, 'tensor', ('engine', 'fsdp')), may hold values from -0.29882812 to 0.29882812
- cache_keys: bfloat16 [64, 512, 128], P(('engine', 'fsdp')), may hold values from -250 to 250
- cache_values: bfloat16 [64, 512, 128], P(('engine', 'fsdp')), may hold values from -6 to 6
- positions: int32 [64, 128], P(('engine', 'fsdp')), may hold values from 0 to 767, as said below
- offsets: int32 [64], P(('engine', 'fsdp')), may hold values from 0 to 512, as said below
Outputs:
- attended: bfloat16 [8192, 16384], P(('engine', 'fsdp'), 'tensor')
The draws below stay inside these ranges and needn't reach their ends.
Inputs may be any that keep to these rules, and one draw needn't show every extreme that they name: `offsets`: each group's offset is its count of valid cache slots; some group has 512 and some group has 0. `positions`: positions rise along each group's row, by 1 or 2 a token; the first is its group's offset or one more; the group with 512 valid slots rises by 2 at every token.
All inputs are finite; a program needn't handle non-finite values.
Results may differ from the reference program's by a relative error of at most 0.03.
Values may be sent and summed in bfloat16 or wider, within the bound.
No kernel may reach another device: no remote copies, remote signals or barrier semaphores. Data moves between devices by JAX's collectives and lax.ppermute only.
A program may use at most 64 MiB of HBM per device.

```python
import jax
import jax.numpy as jnp
from jax import lax

MODEL_WIDTH = 16384
HEAD = 128
RANK = 64
TOK = 128
CACHE = 512
GROUPS = 64
QHEADS = 8
QUERY_FEATURES = 1024
DBLOCK = 2048
TOKENS = 8192
N_TENSOR = 8


def shared_offsets(key):
    counts = jax.random.randint(jax.random.fold_in(key, 11), (GROUPS,), 0, CACHE + 1)
    full_group = jax.random.randint(jax.random.fold_in(key, 12), (), 0, GROUPS)
    empty_group = (full_group + 1 + jax.random.randint(jax.random.fold_in(key, 13), (), 0, GROUPS - 1)) % GROUPS
    counts = counts.at[full_group].set(CACHE)
    counts = counts.at[empty_group].set(0)
    return (counts.astype(jnp.int32), full_group)


def draw_offsets(key, part):
    counts, full_group = shared_offsets(key)
    return counts


def draw_positions(key, part):
    starts, full_group = shared_offsets(key)
    key = jax.random.fold_in(key, 5)
    strides = jax.random.randint(key, (GROUPS, TOK), 1, 3)
    chosen = (jnp.arange(GROUPS) == full_group)[:, None]
    strides = jnp.where(chosen, 2, strides)
    return (starts[:, None] + jnp.cumsum(strides, axis=1) - 1).astype(jnp.int32)


def draw_cache_keys(key, part):
    key = jax.random.fold_in(key, 7)
    base = jnp.clip(jax.random.normal(key, (GROUPS, CACHE, HEAD), jnp.float32), -6.0, 6.0)
    return base.astype(jnp.bfloat16)


def block_levels(stream_key, shape, split, smallest, largest):
    level = 1.0
    for axis_at, blocks in split:
        steps = jax.random.uniform(jax.random.fold_in(jax.random.fold_in(stream_key, 6), axis_at), (blocks,), jnp.float32, smallest / len(split), largest / len(split))
        level = level * jnp.repeat(jnp.exp(steps), shape[axis_at] // blocks).reshape((-1,) + (1,) * (len(shape) - 1 - axis_at))
    return level


def scatter_about(rng, extent, spread, limit, shards=(), kind=jnp.bfloat16):
    values = jax.random.normal(rng, extent, jnp.float32) * spread
    if len(shards) > 0:
        values = block_levels(rng, extent, shards, -0.22, 0.18) * values
    return jnp.clip(values, min=-limit, max=limit).astype(kind)


def setup_inputs(seed: int = 0) -> dict:
    seeds = jax.random.split(jax.random.key(seed), 14)
    return {
        "layer_input": scatter_about(seeds[0], (TOKENS, MODEL_WIDTH), 1.0, 6.0, ((0, 64), (1, 8))),
        "norm_gain": jnp.clip(1.0 + 0.18 * jax.random.normal(seeds[1], (MODEL_WIDTH,), jnp.float32), 0.099609375, 1.8984375).astype(jnp.bfloat16),
        "query_base": scatter_about(seeds[2], (MODEL_WIDTH, QUERY_FEATURES), MODEL_WIDTH ** -0.5, 0.046875, ((0, 64), (1, 8))),
        "query_down": scatter_about(seeds[3], (MODEL_WIDTH, RANK), MODEL_WIDTH ** -0.5, 0.046875, ((0, 64),)),
        "query_up": scatter_about(seeds[4], (RANK, QUERY_FEATURES), 0.05, 0.29882812, ((1, 8),)),
        "kv_base": scatter_about(seeds[5], (N_TENSOR, DBLOCK, 2 * HEAD), MODEL_WIDTH ** -0.5, 0.046875, ((0, 8), (1, 64))),
        "output_base_weight": scatter_about(seeds[6], (QUERY_FEATURES, N_TENSOR, DBLOCK), QUERY_FEATURES ** -0.5, 0.1875, ((1, 8), (2, 64))),
        "output_down_factor": scatter_about(seeds[7], (QUERY_FEATURES, RANK), QUERY_FEATURES ** -0.5, 0.1875, ((0, 8),)),
        "output_up_factor": scatter_about(seeds[8], (RANK, N_TENSOR, DBLOCK), 0.05, 0.29882812, ((1, 8), (2, 64))),
        "cache_keys": draw_cache_keys(jax.random.fold_in(seeds[13], 71), 0),
        "cache_values": scatter_about(seeds[10], (GROUPS, CACHE, HEAD), 1.0, 6.0, ((0, 64),)),
        "positions": draw_positions(jax.random.fold_in(seeds[13], 71), 0),
        "offsets": draw_offsets(jax.random.fold_in(seeds[13], 71), 0),
    }


def rotate(values, places):
    half = values.shape[-1] // 2
    index = jnp.arange(half).astype(jnp.float32)
    inverse = jnp.exp(index * (-2.0 / values.shape[-1]) * jnp.log(jnp.float32(500000.0)))
    angle = places.astype(jnp.float32)[:, None] * inverse[None, :]
    cosine = jnp.cos(angle)
    sine = jnp.sin(angle)
    first = values[:, :half]
    second = values[:, half:]
    return jnp.concatenate([first * cosine - second * sine, second * cosine + first * sine], axis=1)

def attend(query, new_keys, new_values, old_keys, old_values, offset):
    tok_count = query.shape[0]
    slots = old_keys.shape[0]
    keys_all = jnp.concatenate([old_keys, new_keys], axis=0)
    values_all = jnp.concatenate([old_values, new_values], axis=0)
    scores = jnp.dot(query, keys_all.T, preferred_element_type=jnp.float32) * query.shape[-1] ** (-0.5)
    slot_seen = jnp.broadcast_to(jnp.arange(slots)[None, :] < offset, (tok_count, slots))
    rows = jnp.arange(tok_count)
    new_seen = rows[None, :] <= rows[:, None]
    seen = jnp.concatenate([slot_seen, new_seen], axis=1)
    scores = jnp.where(seen, scores, jnp.float32(-1e+30))
    top = lax.optimization_barrier(jnp.max(scores, axis=1, keepdims=True))
    probs = jnp.exp(scores - top)
    weights = (probs / lax.optimization_barrier(jnp.sum(probs, axis=1, keepdims=True))).astype(jnp.bfloat16)
    return jnp.dot(weights, values_all, preferred_element_type=jnp.float32).astype(jnp.bfloat16)

def reference(layer_input, norm_gain, query_base, query_down, query_up, kv_base, output_base_weight, output_down_factor, output_up_factor, cache_keys, cache_values, positions, offsets):
    query_merged = (query_base.astype(jnp.float32) + 2.0 * jnp.dot(query_down, query_up, preferred_element_type=jnp.float32)).astype(jnp.bfloat16)
    adapter_output_delta = jnp.einsum('lz,zam->lam', output_down_factor.astype(jnp.float32), output_up_factor.astype(jnp.float32))
    output_weight_combined = (output_base_weight.astype(jnp.float32) + 2.0 * adapter_output_delta).astype(jnp.bfloat16).reshape(QUERY_FEATURES, MODEL_WIDTH)
    kv_weight = kv_base.reshape(MODEL_WIDTH, 2 * HEAD)
    inputs = layer_input.reshape(GROUPS, TOK, MODEL_WIDTH)

    def one_group(packed):
        block, old_keys, old_values, places, offset = packed
        wide = block.astype(jnp.float32)
        scale = lax.rsqrt(lax.optimization_barrier(jnp.mean(wide * wide, axis=1, keepdims=True)) + 1e-05)
        normed = (wide * scale * norm_gain.astype(jnp.float32)[None, :]).astype(jnp.bfloat16)
        query_all = jnp.dot(normed, query_merged, preferred_element_type=jnp.float32)
        kv = jnp.dot(normed, kv_weight, preferred_element_type=jnp.float32)
        new_keys = rotate(kv[:, :HEAD], places).astype(jnp.bfloat16)
        new_values = kv[:, HEAD:].astype(jnp.bfloat16)
        total = jnp.zeros((TOK, MODEL_WIDTH), jnp.float32)
        for head in range(QHEADS):
            query = rotate(query_all[:, head * HEAD:(head + 1) * HEAD], places).astype(jnp.bfloat16)
            head_out = attend(query, new_keys, new_values, old_keys, old_values, offset)
            part = jnp.dot(head_out, output_weight_combined[head * HEAD:(head + 1) * HEAD], preferred_element_type=jnp.float32)
            total = total + part.astype(jnp.bfloat16).astype(jnp.float32)
        return total.astype(jnp.bfloat16)
    result = lax.map(one_group, (inputs, cache_keys, cache_values, positions, offsets))
    return result.reshape(TOKENS, MODEL_WIDTH)
```

```python
import jax
import jax.numpy as jnp
from jax import lax
from jax.sharding import PartitionSpec as P

AXES = ("engine", "fsdp", "tensor")


def rotate(values, places):
    half = values.shape[-1] // 2
    index = jnp.arange(half).astype(jnp.float32)
    inverse = jnp.exp(index * (-2.0 / values.shape[-1]) * jnp.log(jnp.float32(500000.0)))
    angle = places.astype(jnp.float32)[:, None] * inverse[None, :]
    cosine = jnp.cos(angle)
    sine = jnp.sin(angle)
    first = values[:, :half]
    second = values[:, half:]
    return jnp.concatenate([first * cosine - second * sine, second * cosine + first * sine], axis=1)


def attend(query, new_keys, new_values, old_keys, old_values, offset):
    tok_count = query.shape[0]
    slots = old_keys.shape[0]
    keys_all = jnp.concatenate([old_keys, new_keys], axis=0)
    values_all = jnp.concatenate([old_values, new_values], axis=0)
    scores = jnp.dot(query, keys_all.T, preferred_element_type=jnp.float32) * query.shape[-1] ** (
        -0.5
    )
    slot_seen = jnp.broadcast_to(jnp.arange(slots)[None, :] < offset, (tok_count, slots))
    rows = jnp.arange(tok_count)
    new_seen = rows[None, :] <= rows[:, None]
    seen = jnp.concatenate([slot_seen, new_seen], axis=1)
    scores = jnp.where(seen, scores, jnp.float32(-1e30))
    top = jnp.max(scores, axis=1, keepdims=True)
    probs = jnp.exp(scores - top)
    weights = (probs / jnp.sum(probs, axis=1, keepdims=True)).astype(jnp.bfloat16)
    return jnp.dot(weights, values_all, preferred_element_type=jnp.float32).astype(jnp.bfloat16)


def shard_home(e, f, t):
    z, y = f // 2, f % 2
    return t // 2, ((t % 2) * 4 + z % 4) * 2 + y, e * 2 + z // 4


def swap_engine(e, f, t):
    return t // 2, f, e * 2 + t % 2


def pairs(move):
    flat = lambda e, f, t: (e * 16 + f) * 8 + t
    return [
        (flat(e, f, t), flat(*move(e, f, t)))
        for e in range(4)
        for f in range(16)
        for t in range(8)
    ]


def per_device(
    layer_input,
    norm_gain,
    query_base,
    query_down,
    query_up,
    kv_base,
    output_base_weight,
    output_down_factor,
    output_up_factor,
    cache_keys,
    cache_values,
    positions,
    offsets,
):
    engine = lax.axis_index("engine")
    merged_query = (
        query_base.astype(jnp.float32)
        + 2.0 * jnp.dot(query_down, query_up, preferred_element_type=jnp.float32)
    ).astype(jnp.bfloat16)
    query_shard = lax.ppermute(merged_query, AXES, pairs(shard_home))

    keys_half, values_half = kv_base[0, :, :128], kv_base[0, :, 128:]
    kv_parts = jnp.stack([keys_half, keys_half, values_half, values_half])
    kv_parts = lax.all_to_all(kv_parts, "engine", split_axis=0, concat_axis=0, tiled=True)
    kv_shard = lax.dynamic_slice_in_dim(kv_parts, (engine % 2) * 2, 2, axis=0).reshape(64, 128)

    shard = jnp.concatenate([query_shard, kv_shard], axis=0)
    gathered = lax.all_to_all(
        jnp.broadcast_to(shard[None], (16, 320, 128)), "fsdp", split_axis=0, concat_axis=0, tiled=True
    )

    wide = layer_input.astype(jnp.float32)
    squares = lax.all_gather(jnp.sum(wide * wide, axis=1)[None], "tensor", axis=0, tiled=True)
    scale = lax.rsqrt(jnp.sum(squares, axis=0) / 16384.0 + 1e-05)
    normed = (wide * scale[:, None] * norm_gain.astype(jnp.float32)[None, :]).astype(jnp.bfloat16)
    tokens = lax.all_gather(normed, "engine", axis=0, tiled=True)

    query_weight = gathered[:, :256].reshape(2, 2048, 128)
    kv_weight = gathered[:, 256:].reshape(16, 2, 32, 128).transpose(1, 0, 2, 3).reshape(1024, 128)
    some_tokens = lax.dynamic_slice_in_dim(tokens, (engine % 2) * 1024, 1024, axis=1)
    kv_terms = jnp.dot(some_tokens, kv_weight, preferred_element_type=jnp.float32)
    kv_terms = kv_terms.astype(jnp.bfloat16).reshape(4, 1, 128, 128)
    query_terms = jnp.stack(
        [
            jnp.dot(tokens, query_weight[c], preferred_element_type=jnp.float32)
            .astype(jnp.bfloat16)
            .reshape(4, 128, 128)
            for c in range(2)
        ],
        axis=1,
    )
    terms = jnp.concatenate([query_terms, jnp.broadcast_to(kv_terms, (4, 2, 128, 128))], axis=3)
    terms = lax.all_to_all(
        terms.reshape(8, 128, 256), "tensor", split_axis=0, concat_axis=0, tiled=True
    )
    total = jnp.sum(terms.astype(jnp.float32), axis=0)
    kv_all = lax.all_gather(total[:, 128:], "engine", axis=0, tiled=True).reshape(4, 128, 128)

    old = lax.ppermute(jnp.stack([cache_keys[0], cache_values[0]]), AXES, pairs(swap_engine))
    numbers = jnp.concatenate([positions[0], jnp.broadcast_to(offsets, (128,))]).reshape(2, 128)
    numbers = lax.ppermute(numbers, AXES, pairs(swap_engine))
    places = numbers[0]
    query = rotate(total[:, :128], places).astype(jnp.bfloat16)
    new_keys = rotate(kv_all[0] + kv_all[1], places).astype(jnp.bfloat16)
    new_values = (kv_all[2] + kv_all[3]).astype(jnp.bfloat16)
    head_out = attend(query, new_keys, new_values, old[0], old[1], numbers[1, 0])

    down = lax.all_gather(output_down_factor, "tensor", axis=0, tiled=True)
    up = output_up_factor[:, 0, :]
    delta = lax.dot_general(up, down, (((0,), (1,)), ((), ())), preferred_element_type=jnp.float32)
    out_shard = (output_base_weight[:, 0, :].T.astype(jnp.float32) + 2.0 * delta).astype(jnp.bfloat16)
    out_weight = lax.all_gather(out_shard, "fsdp", axis=0, tiled=True)

    heads = lax.all_gather(head_out[None], "tensor", axis=0, tiled=True)
    heads = lax.all_gather(heads[None], "engine", axis=0, tiled=True)
    heads = heads.reshape(4, 4, 2, 128, 128).transpose(1, 3, 0, 2, 4).reshape(512, 1024)
    out = lax.dot_general(
        heads, out_weight, (((1,), (1,)), ((), ())), preferred_element_type=jnp.float32
    ).astype(jnp.bfloat16)
    out = lax.all_to_all(
        out.reshape(4, 128, 512), "engine", split_axis=0, concat_axis=0, tiled=True
    )
    return out.transpose(1, 0, 2).reshape(128, 2048)


def solution(mesh):
    in_specs = (
        P(("engine", "fsdp"), "tensor"),
        P("tensor"),
        P(("engine", "fsdp"), "tensor"),
        P(("engine", "fsdp"), None),
        P(None, "tensor"),
        P("tensor", ("engine", "fsdp"), None),
        P(None, "tensor", ("engine", "fsdp")),
        P("tensor", None),
        P(None, "tensor", ("engine", "fsdp")),
        P(("engine", "fsdp"), None, None),
        P(("engine", "fsdp"), None, None),
        P(("engine", "fsdp"), None),
        P(("engine", "fsdp")),
    )
    out_specs = P(("engine", "fsdp"), "tensor")
    return jax.shard_map(
        per_device, mesh=mesh, in_specs=in_specs, out_specs=out_specs, check_vma=False
    )
```

```python
import jax
import jax.numpy as jnp
from jax import lax
from jax.sharding import PartitionSpec as P

AXES = ("engine", "fsdp", "tensor")


def rotate(values, places):
    half = values.shape[-1] // 2
    index = jnp.arange(half).astype(jnp.float32)
    inverse = jnp.exp(index * (-2.0 / values.shape[-1]) * jnp.log(jnp.float32(500000.0)))
    angle = places.astype(jnp.float32)[:, None] * inverse[None, :]
    cosine = jnp.cos(angle)
    sine = jnp.sin(angle)
    first = values[:, :half]
    second = values[:, half:]
    return jnp.concatenate([first * cosine - second * sine, second * cosine + first * sine], axis=1)


def attend(query, new_keys, new_values, old_keys, old_values, offset):
    tok_count = query.shape[0]
    slots = old_keys.shape[0]
    keys_all = jnp.concatenate([old_keys, new_keys], axis=0)
    values_all = jnp.concatenate([old_values, new_values], axis=0)
    scores = jnp.dot(query, keys_all.T, preferred_element_type=jnp.float32) * query.shape[-1] ** (
        -0.5
    )
    slot_seen = jnp.broadcast_to(jnp.arange(slots)[None, :] < offset, (tok_count, slots))
    rows = jnp.arange(tok_count)
    new_seen = rows[None, :] <= rows[:, None]
    seen = jnp.concatenate([slot_seen, new_seen], axis=1)
    scores = jnp.where(seen, scores, jnp.float32(-1e30))
    top = jnp.max(scores, axis=1, keepdims=True)
    probs = jnp.exp(scores - top)
    weights = (probs / jnp.sum(probs, axis=1, keepdims=True)).astype(jnp.bfloat16)
    return jnp.dot(weights, values_all, preferred_element_type=jnp.float32).astype(jnp.bfloat16)


def shard_home(e, f, t):
    z, y = f // 2, f % 2
    return t // 2, ((t % 2) * 4 + z % 4) * 2 + y, e * 2 + z // 4


def swap_engine(e, f, t):
    return t // 2, f, e * 2 + t % 2


def pairs(move):
    flat = lambda e, f, t: (e * 16 + f) * 8 + t
    return [
        (flat(e, f, t), flat(*move(e, f, t)))
        for e in range(4)
        for f in range(16)
        for t in range(8)
    ]


def per_device(
    layer_input,
    norm_gain,
    query_base,
    query_down,
    query_up,
    kv_base,
    output_base_weight,
    output_down_factor,
    output_up_factor,
    cache_keys,
    cache_values,
    positions,
    offsets,
):
    engine = lax.axis_index("engine")
    tokens = lax.all_gather(layer_input, "engine", axis=0, tiled=True)

    merged_query = (
        query_base.astype(jnp.float32)
        + 2.0 * jnp.dot(query_down, query_up, preferred_element_type=jnp.float32)
    ).astype(jnp.bfloat16)
    query_shard = lax.ppermute(merged_query, AXES, pairs(shard_home))

    keys_half, values_half = kv_base[0, :, :128], kv_base[0, :, 128:]
    kv_parts = jnp.stack([keys_half, keys_half, values_half, values_half])
    kv_parts = lax.all_to_all(kv_parts, "engine", split_axis=0, concat_axis=0, tiled=True)
    kv_shard = lax.dynamic_slice_in_dim(kv_parts, (engine % 2) * 2, 2, axis=0).reshape(64, 128)

    shard = jnp.concatenate([query_shard, kv_shard], axis=0)
    gathered = lax.all_to_all(
        jnp.broadcast_to(shard[None], (16, 320, 128)), "fsdp", split_axis=0, concat_axis=0, tiled=True
    )

    numbers = jnp.concatenate([positions, jnp.broadcast_to(offsets[:, None], (1, 128))])
    numbers = jnp.concatenate([numbers // 256, numbers % 256, jnp.zeros((12, 128), jnp.int32)])
    group = jnp.concatenate([cache_keys[0], cache_values[0], numbers.astype(jnp.bfloat16)])
    group = lax.ppermute(group, AXES, pairs(swap_engine))

    down = lax.all_gather(output_down_factor, "tensor", axis=0, tiled=True)
    up = output_up_factor[:, 0, :]
    delta = lax.dot_general(up, down, (((0,), (1,)), ((), ())), preferred_element_type=jnp.float32)
    out_shard = (output_base_weight[:, 0, :].T.astype(jnp.float32) + 2.0 * delta).astype(jnp.bfloat16)
    gathered, _, group = lax.optimization_barrier((gathered, out_shard, group))
    out_weight = lax.all_gather(out_shard, "fsdp", axis=0, tiled=True)

    wide = tokens.astype(jnp.float32)
    scaled = (wide * norm_gain.astype(jnp.float32)[None, :]).astype(jnp.bfloat16)
    squares = jnp.sum(wide * wide, axis=1).reshape(4, 1, 1, 128)
    squares_high = squares.astype(jnp.bfloat16)
    squares_low = (squares - squares_high.astype(jnp.float32)).astype(jnp.bfloat16)
    squares = jnp.concatenate([squares_high, squares_low], axis=3)

    query_weight = gathered[:, :256].reshape(2, 2048, 128)
    kv_weight = gathered[:, 256:].reshape(16, 2, 32, 128).transpose(1, 0, 2, 3).reshape(1024, 128)
    some_tokens = lax.dynamic_slice_in_dim(scaled, (engine % 2) * 1024, 1024, axis=1)
    kv_terms = jnp.dot(some_tokens, kv_weight, preferred_element_type=jnp.float32)
    kv_terms = kv_terms.astype(jnp.bfloat16).reshape(4, 1, 128, 128)
    query_terms = jnp.stack(
        [
            jnp.dot(scaled, query_weight[c], preferred_element_type=jnp.float32)
            .astype(jnp.bfloat16)
            .reshape(4, 128, 128)
            for c in range(2)
        ],
        axis=1,
    )
    terms = jnp.concatenate([query_terms, jnp.broadcast_to(kv_terms, (4, 2, 128, 128))], axis=3)
    terms = jnp.concatenate([terms, jnp.broadcast_to(squares, (4, 2, 8, 256))], axis=2)
    terms = lax.all_to_all(
        terms.reshape(8, 136, 256), "tensor", split_axis=0, concat_axis=0, tiled=True
    )
    total = jnp.sum(terms.astype(jnp.float32), axis=0)
    mean = (total[128, :128] + total[128, 128:]) / 16384.0
    total = total[:128] * lax.rsqrt(mean + 1e-05)[:, None]
    kv_all = lax.all_gather(total[:, 128:], "engine", axis=0, tiled=True).reshape(4, 128, 128)

    numbers = group[1024:].astype(jnp.float32)
    numbers = (numbers[0:2] * 256.0 + numbers[2:4]).astype(jnp.int32)
    places = numbers[0]
    query = rotate(total[:, :128], places).astype(jnp.bfloat16)
    new_keys = rotate(kv_all[0] + kv_all[1], places).astype(jnp.bfloat16)
    new_values = (kv_all[2] + kv_all[3]).astype(jnp.bfloat16)
    head_out = attend(query, new_keys, new_values, group[:512], group[512:1024], numbers[1, 0])

    heads = lax.all_gather(head_out[None], "tensor", axis=0, tiled=True)
    heads = lax.all_to_all(
        jnp.broadcast_to(heads[None], (4, 8, 128, 128)), "engine", split_axis=0, concat_axis=0, tiled=True
    )
    heads = heads.reshape(4, 4, 2, 128, 128).transpose(1, 3, 0, 2, 4).reshape(512, 1024)
    out = lax.dot_general(
        heads, out_weight, (((1,), (1,)), ((), ())), preferred_element_type=jnp.float32
    ).astype(jnp.bfloat16)
    out = lax.all_to_all(
        out.reshape(4, 128, 512), "engine", split_axis=0, concat_axis=0, tiled=True
    )
    return out.transpose(1, 0, 2).reshape(128, 2048)


def solution(mesh):
    in_specs = (
        P(("engine", "fsdp"), "tensor"),
        P("tensor"),
        P(("engine", "fsdp"), "tensor"),
        P(("engine", "fsdp"), None),
        P(None, "tensor"),
        P("tensor", ("engine", "fsdp"), None),
        P(None, "tensor", ("engine", "fsdp")),
        P("tensor", None),
        P(None, "tensor", ("engine", "fsdp")),
        P(("engine", "fsdp"), None, None),
        P(("engine", "fsdp"), None, None),
        P(("engine", "fsdp"), None),
        P(("engine", "fsdp")),
    )
    out_specs = P(("engine", "fsdp"), "tensor")
    return jax.shard_map(
        per_device, mesh=mesh, in_specs=in_specs, out_specs=out_specs, check_vma=False
    )
```

```python
import jax
import jax.numpy as jnp
from jax import lax
from jax.experimental import pallas as pl
from jax.experimental.pallas import tpu as pltpu
from jax.sharding import PartitionSpec as P

AXES = ("engine", "fsdp", "tensor")


def rotate(values, places):
    half = values.shape[-1] // 2
    index = jnp.arange(half).astype(jnp.float32)
    inverse = jnp.exp(index * (-2.0 / values.shape[-1]) * jnp.log(jnp.float32(500000.0)))
    angle = places.astype(jnp.float32)[:, None] * inverse[None, :]
    cosine = jnp.cos(angle)
    sine = jnp.sin(angle)
    first = values[:, :half]
    second = values[:, half:]
    return jnp.concatenate([first * cosine - second * sine, second * cosine + first * sine], axis=1)


def attend(query, new_keys, new_values, old_keys, old_values, offset):
    tok_count = query.shape[0]
    slots = old_keys.shape[0]
    keys_all = jnp.concatenate([old_keys, new_keys], axis=0)
    values_all = jnp.concatenate([old_values, new_values], axis=0)
    scores = jnp.dot(query, keys_all.T, preferred_element_type=jnp.float32) * query.shape[-1] ** (
        -0.5
    )
    slot_seen = jnp.broadcast_to(jnp.arange(slots)[None, :] < offset, (tok_count, slots))
    rows = jnp.arange(tok_count)
    new_seen = rows[None, :] <= rows[:, None]
    seen = jnp.concatenate([slot_seen, new_seen], axis=1)
    scores = jnp.where(seen, scores, jnp.float32(-1e30))
    top = jnp.max(scores, axis=1, keepdims=True)
    probs = jnp.exp(scores - top)
    weights = (probs / jnp.sum(probs, axis=1, keepdims=True)).astype(jnp.bfloat16)
    return jnp.dot(weights, values_all, preferred_element_type=jnp.float32).astype(jnp.bfloat16)


ACROSS = [[0, 2, 4, 6], [1, 3, 5, 7]]
ALONG_Z = [[2 * z + y for z in range(8)] for y in range(2)]


def shard_home(e, f, t):
    z, y = f // 2, f % 2
    return t // 2, (((t % 2) ^ (z // 4)) * 4 + z % 4) * 2 + y, e * 2 + z // 4


def other_core(e, f, t):
    return e, f, t ^ 1


def other_y(e, f, t):
    return e, f ^ 1, t


def next_engine(e, f, t):
    return (e + 1) % 4, f, t


def last_engine(e, f, t):
    return (e + 3) % 4, f, t


def move(array, where):
    flat = lambda e, f, t: (e * 16 + f) * 8 + t
    pairs = [
        (flat(e, f, t), flat(*where(e, f, t)))
        for e in range(4)
        for f in range(16)
        for t in range(8)
    ]
    return lax.ppermute(array, AXES, pairs)


def from_engines(array):
    half = array.shape[0] // 2
    before, after = move(array, next_engine), move(array, last_engine)
    across_low, across_high = move(before[:half], next_engine), move(after[half:], last_engine)
    return array, after, across_low, across_high, before


def exchange(array, axis, groups=None):
    return lax.all_to_all(
        array, axis, split_axis=0, concat_axis=0, tiled=True, axis_index_groups=groups
    )


def spread(array, axis, groups=None):
    return exchange(jnp.broadcast_to(array[None], (4, *array.shape)), axis, groups)


def split(sums):
    high = sums.astype(jnp.bfloat16)
    return jnp.concatenate([high, (sums - high.astype(jnp.float32)).astype(jnp.bfloat16)], axis=1)


def project_kernel(place_ref, own_ref, other_ref, own_w, after_w, low_w, high_w, before_w, out_ref):
    engine, core = place_ref[0], place_ref[1]
    rows = []
    for i in range(4):
        own, other = own_ref[i], other_ref[i]
        rows += [jnp.where(core == 0, own, other), jnp.where(core == 0, other, own)]
    rows = jnp.concatenate(rows, axis=1)
    heads, down = rows[:128], rows[128:]
    inner = (((1,), (1,)), ((), ()))
    mixed = lax.dot_general(heads, down, inner, preferred_element_type=jnp.float32)
    mixed = (2.0 * mixed).astype(jnp.bfloat16)
    for weight_ref, step, start in (
        (own_w, 0, 0),
        (after_w, 1, 0),
        (low_w, 2, 0),
        (high_w, 2, 256),
        (before_w, 3, 0),
    ):
        width = weight_ref.shape[0]
        out = lax.dot_general(
            heads, weight_ref[:, :1024], inner, preferred_element_type=jnp.float32
        ) + lax.dot_general(
            mixed, weight_ref[:, 1024:1088], inner, preferred_element_type=jnp.float32
        )
        place = pl.multiple_of(lax.rem(engine + step, 4) * 512 + start, 256)
        out_ref[:, pl.ds(place, width)] = out.astype(jnp.bfloat16)


def project(place, own, other, weights):
    return pl.pallas_call(
        project_kernel,
        out_shape=jax.ShapeDtypeStruct((128, 2048), jnp.bfloat16),
        in_specs=[pl.BlockSpec(memory_space=pltpu.SMEM)]
        + [pl.BlockSpec(memory_space=pltpu.VMEM)] * 7,
        out_specs=pl.BlockSpec(memory_space=pltpu.VMEM),
        compiler_params=pltpu.CompilerParams(vmem_limit_bytes=24 * 2**20),
    )(place, own, other, *weights)


def per_device(
    layer_input,
    norm_gain,
    query_base,
    query_down,
    query_up,
    kv_base,
    output_base_weight,
    output_down_factor,
    output_up_factor,
    cache_keys,
    cache_values,
    positions,
    offsets,
):
    engine = lax.axis_index("engine")
    fsdp = lax.axis_index("fsdp")
    core = lax.axis_index("tensor") % 2

    merged_query = (
        query_base.astype(jnp.float32)
        + 2.0 * jnp.dot(query_down, query_up, preferred_element_type=jnp.float32)
    ).astype(jnp.bfloat16)
    merged_query, kv_base = lax.optimization_barrier((merged_query, kv_base))
    query_shard = move(merged_query, shard_home)

    out_shard = jnp.concatenate(
        [output_base_weight[:, 0, :].T, output_up_factor[:, 0, :].T, jnp.zeros((32, 64), jnp.bfloat16)],
        axis=1,
    )
    out_other = move(out_shard, other_y)
    first = fsdp % 2 == 0
    out_shard = jnp.concatenate(
        [jnp.where(first, out_shard, out_other), jnp.where(first, out_other, out_shard)], axis=0
    )
    out_weight = lax.all_gather(out_shard, "fsdp", axis=0, tiled=True, axis_index_groups=ALONG_Z)

    keys_half, values_half = kv_base[0, :, :128], kv_base[0, :, 128:]
    kv_parts = exchange(jnp.stack([keys_half, keys_half, values_half, values_half]), "engine")
    kv_shard = lax.dynamic_slice_in_dim(kv_parts, (engine % 2) * 2, 2, axis=0).reshape(64, 128)

    shard = jnp.concatenate([query_shard, kv_shard], axis=0)
    shards = jnp.broadcast_to(shard[None], (16, 320, 128))
    shards, layer_input = lax.optimization_barrier((shards, layer_input))
    gathered = exchange(shards, "fsdp")

    wide = layer_input.astype(jnp.float32)
    squares = jnp.sum(wide * wide, axis=1)[None]
    scaled = (wide * norm_gain.astype(jnp.float32)[None, :]).astype(jnp.bfloat16)
    tokens = jnp.concatenate(from_engines(scaled), axis=0)
    out_weights = from_engines(out_weight)
    gathered, tokens, squares = lax.optimization_barrier((gathered, tokens, squares))

    query_weight = gathered[:, :256].reshape(2, 2048, 128)
    kv_weight = gathered[:, 256:].reshape(16, 2, 32, 128).transpose(1, 0, 2, 3).reshape(1024, 128)
    some_tokens = lax.dynamic_slice_in_dim(tokens, (engine % 2) * 1024, 1024, axis=1)
    terms = [
        jnp.dot(tokens, query_weight[0], preferred_element_type=jnp.float32),
        jnp.dot(tokens, query_weight[1], preferred_element_type=jnp.float32),
        jnp.dot(some_tokens, kv_weight, preferred_element_type=jnp.float32),
    ]
    terms = jnp.concatenate([term.astype(jnp.bfloat16) for term in terms], axis=1)
    terms = terms.reshape(4, 128, 384)
    terms = lax.dynamic_slice_in_dim(jnp.concatenate([terms, terms]), 4 - engine, 4, axis=0)
    terms = exchange(terms, "engine").astype(jnp.float32)
    kv_terms = jnp.concatenate(
        [terms[0, :, 256:] + terms[1, :, 256:], terms[2, :, 256:] + terms[3, :, 256:]], axis=1
    )
    own = jnp.concatenate([terms[i, :, :128] for i in range(4)] + [kv_terms], axis=1)
    other = jnp.concatenate([terms[i, :, 128:256] for i in range(4)] + [kv_terms], axis=1)
    given = jnp.concatenate(
        [other.astype(jnp.bfloat16), jnp.tile(split(squares), (8, 3))], axis=0
    )
    given = move(given, other_core).astype(jnp.float32)
    own = (own + given[:128]).astype(jnp.bfloat16)
    squares = squares + given[128:129, :128] + given[128:129, 128:256]
    squares = jnp.tile(split(squares), (1, 2))[:, :384]
    terms = jnp.stack(
        [
            jnp.concatenate(
                [
                    jnp.concatenate([own[:, i * 128 : (i + 1) * 128], own[:, 512:]], axis=1),
                    jnp.broadcast_to(squares, (8, 384)),
                ],
                axis=0,
            )
            for i in range(4)
        ]
    )
    terms = exchange(terms, "tensor", ACROSS)
    total = jnp.sum(terms.astype(jnp.float32), axis=0)
    mean = (total[128, :128] + total[128, 128:256]) / 16384.0
    total = total[:128] * lax.rsqrt(mean + 1e-05)[:, None]

    places = positions[0]
    query = rotate(total[:, :128], places).astype(jnp.bfloat16)
    new_keys = rotate(total[:, 128:256], places).astype(jnp.bfloat16)
    new_values = total[:, 256:].astype(jnp.bfloat16)
    head_out = attend(query, new_keys, new_values, cache_keys[0], cache_values[0], offsets[0])

    heads = jnp.concatenate([head_out, output_down_factor.T], axis=0)
    own = spread(heads, "tensor", ACROSS)
    other = move(own, other_core)
    place = jnp.stack([engine, core]).astype(jnp.int32)
    return project(place, own, other, out_weights)


def solution(mesh):
    in_specs = (
        P(("engine", "fsdp"), "tensor"),
        P("tensor"),
        P(("engine", "fsdp"), "tensor"),
        P(("engine", "fsdp"), None),
        P(None, "tensor"),
        P("tensor", ("engine", "fsdp"), None),
        P(None, "tensor", ("engine", "fsdp")),
        P("tensor", None),
        P(None, "tensor", ("engine", "fsdp")),
        P(("engine", "fsdp"), None, None),
        P(("engine", "fsdp"), None, None),
        P(("engine", "fsdp"), None),
        P(("engine", "fsdp")),
    )
    out_specs = P(("engine", "fsdp"), "tensor")
    return jax.shard_map(
        per_device, mesh=mesh, in_specs=in_specs, out_specs=out_specs, check_vma=False
    )
```

```python
import jax
import jax.numpy as jnp
from jax import lax
from jax.experimental import pallas as pl
from jax.experimental.pallas import tpu as pltpu
from jax.sharding import PartitionSpec as P

AXES = ("engine", "fsdp", "tensor")


def rotate(values, places):
    half = values.shape[-1] // 2
    index = jnp.arange(half).astype(jnp.float32)
    inverse = jnp.exp(index * (-2.0 / values.shape[-1]) * jnp.log(jnp.float32(500000.0)))
    angle = places.astype(jnp.float32)[:, None] * inverse[None, :]
    cosine = jnp.cos(angle)
    sine = jnp.sin(angle)
    first = values[:, :half]
    second = values[:, half:]
    return jnp.concatenate([first * cosine - second * sine, second * cosine + first * sine], axis=1)


def attend(query, new_keys, new_values, old_keys, old_values, offset):
    tok_count = query.shape[0]
    slots = old_keys.shape[0]
    keys_all = jnp.concatenate([old_keys, new_keys], axis=0)
    values_all = jnp.concatenate([old_values, new_values], axis=0)
    scores = jnp.dot(query, keys_all.T, preferred_element_type=jnp.float32) * query.shape[-1] ** (
        -0.5
    )
    slot_seen = jnp.broadcast_to(jnp.arange(slots)[None, :] < offset, (tok_count, slots))
    rows = jnp.arange(tok_count)
    new_seen = rows[None, :] <= rows[:, None]
    seen = jnp.concatenate([slot_seen, new_seen], axis=1)
    scores = jnp.where(seen, scores, jnp.float32(-1e30))
    top = jnp.max(scores, axis=1, keepdims=True)
    probs = jnp.exp(scores - top)
    weights = (probs / jnp.sum(probs, axis=1, keepdims=True)).astype(jnp.bfloat16)
    return jnp.dot(weights, values_all, preferred_element_type=jnp.float32).astype(jnp.bfloat16)


ACROSS = [[0, 2, 4, 6], [1, 3, 5, 7]]
CORES = [[0, 1], [2, 3], [4, 5], [6, 7]]
ALONG_Z = [[2 * z + y for z in range(8)] for y in range(2)]


def shard_home(e, f, t):
    z, y = f // 2, f % 2
    home = z if t % 2 == z // 4 else 7 - z
    return t // 2, home * 2 + y, e * 2 + z // 4


def other_core(e, f, t):
    return e, f, t ^ 1


def other_y(e, f, t):
    return e, f ^ 1, t


def next_engine(e, f, t):
    return (e + 1) % 4, f, t


def last_engine(e, f, t):
    return (e + 3) % 4, f, t


def move(array, where):
    flat = lambda e, f, t: (e * 16 + f) * 8 + t
    pairs = [
        (flat(e, f, t), flat(*where(e, f, t)))
        for e in range(4)
        for f in range(16)
        for t in range(8)
    ]
    return lax.ppermute(array, AXES, pairs)


def exchange(array, axis, groups=None):
    return lax.all_to_all(
        array, axis, split_axis=0, concat_axis=0, tiled=True, axis_index_groups=groups
    )


def spread(array, count, axis, groups=None):
    return exchange(jnp.broadcast_to(array[None], (count, *array.shape)), axis, groups)


def split(sums):
    high = sums.astype(jnp.bfloat16)
    return jnp.concatenate([high, (sums - high.astype(jnp.float32)).astype(jnp.bfloat16)], axis=1)


def terms_kernel(place_ref, weight_ref, *refs):
    token_refs, out_ref = refs[:-1], refs[-1]
    engine, core = place_ref[0], place_ref[1]
    own = weight_ref[pl.ds(core * 8, 8), :256].reshape(2048, 128)
    other = weight_ref[pl.ds((1 - core) * 8, 8), :256].reshape(4, 512, 128)
    other = jnp.concatenate([other[3 - i] for i in range(4)], axis=0)
    query_weight = jnp.concatenate([own, other], axis=1)
    kv_weight = jnp.concatenate(
        [weight_ref[:, i : i + 32].reshape(512, 128) for i in (256, 288)], axis=1
    )
    some = pl.ds(pl.multiple_of(engine * 512, 512), 512)
    for ref, step, start in zip(token_refs, (0, 1, 2, 2, 3), (0, 0, 0, 64, 0), strict=True):
        rows = ref.shape[0]
        terms = jnp.concatenate(
            [
                jnp.dot(ref[...], query_weight, preferred_element_type=jnp.float32),
                jnp.dot(ref[:, some], kv_weight, preferred_element_type=jnp.float32),
            ],
            axis=1,
        )
        out_ref[lax.rem(engine + step, 4), start : start + rows] = terms.astype(jnp.bfloat16)


def project_kernel(place_ref, own_ref, other_ref, *refs):
    weight_refs, out_ref, weight_ref = refs[:8], refs[8], refs[9]
    engine, core, y = place_ref[0], place_ref[1], place_ref[2]
    rows = []
    for i in range(4):
        own, other = own_ref[i], other_ref[i]
        rows += [jnp.where(core == 0, own, other), jnp.where(core == 0, other, own)]
    rows = jnp.concatenate(rows, axis=1)
    heads, down = rows[:128], rows[128:]
    inner = (((1,), (1,)), ((), ()))
    mixed = lax.dot_general(heads, down, inner, preferred_element_type=jnp.float32)
    mixed = (2.0 * mixed).astype(jnp.bfloat16)
    heads = jnp.concatenate([heads, mixed, jnp.zeros_like(mixed)], axis=1)
    for step in range(4):
        for ref, half in zip(weight_refs[2 * step : 2 * step + 2], (y, 1 - y), strict=True):
            for z in range(8):
                at = pl.multiple_of(z * 64 + half * 32, 32)
                weight_ref[step, pl.ds(at, 32)] = ref[z * 32 : z * 32 + 32]
        out = lax.dot_general(
            heads, weight_ref[step], inner, preferred_element_type=jnp.float32
        )
        place = pl.multiple_of(lax.rem(engine + step, 4) * 512, 512)
        out_ref[:, pl.ds(place, 512)] = out.astype(jnp.bfloat16)


def compute(kernel, shape, place, arrays, scratch=()):
    return pl.pallas_call(
        kernel,
        out_shape=jax.ShapeDtypeStruct(shape, jnp.bfloat16),
        in_specs=[pl.BlockSpec(memory_space=pltpu.SMEM)]
        + [pl.BlockSpec(memory_space=pltpu.VMEM)] * len(arrays),
        out_specs=pl.BlockSpec(memory_space=pltpu.VMEM),
        scratch_shapes=[pltpu.VMEM(sizes, jnp.bfloat16) for sizes in scratch],
        compiler_params=pltpu.CompilerParams(vmem_limit_bytes=24 * 2**20),
    )(place, *arrays)


def per_device(
    layer_input,
    norm_gain,
    query_base,
    query_down,
    query_up,
    kv_base,
    output_base_weight,
    output_down_factor,
    output_up_factor,
    cache_keys,
    cache_values,
    positions,
    offsets,
):
    engine = lax.axis_index("engine")
    core = lax.axis_index("tensor") % 2
    place = jnp.stack([engine, core, lax.axis_index("fsdp") % 2]).astype(jnp.int32)

    merged_query = (
        query_base.astype(jnp.float32)
        + 2.0 * jnp.dot(query_down, query_up, preferred_element_type=jnp.float32)
    ).astype(jnp.bfloat16)
    out_shard = jnp.concatenate(
        [output_base_weight[:, 0, :].T, output_up_factor[:, 0, :].T, jnp.zeros((32, 64), jnp.bfloat16)],
        axis=1,
    )
    merged_query, out_shard = lax.optimization_barrier((merged_query, out_shard))
    query_shard = move(merged_query, shard_home)
    mine = spread(out_shard, 8, "fsdp", ALONG_Z).reshape(256, 1152)

    shard = jnp.concatenate([query_shard, kv_base[0, :, :128], kv_base[0, :, 128:]], axis=0)
    shards = jnp.broadcast_to(shard[None], (16, 320, 128))
    shards, mine, layer_input = lax.optimization_barrier((shards, mine, layer_input))
    gathered = exchange(shards, "fsdp")

    wide = layer_input.astype(jnp.float32)
    squares = jnp.sum(wide * wide, axis=1)[None]
    squares = lax.all_gather(squares, "tensor", axis=0, tiled=True, axis_index_groups=CORES)
    squares = jnp.sum(squares, axis=0, keepdims=True)
    scaled = (wide * norm_gain.astype(jnp.float32)[None, :]).astype(jnp.bfloat16)
    scaled, squares, mine = lax.optimization_barrier((scaled, squares, mine))
    before, after = move(scaled, next_engine), move(scaled, last_engine)
    theirs = move(mine, other_y)
    across_low, across_high = move(before[:64], next_engine), move(after[64:], last_engine)
    tokens = (scaled, after, across_low, across_high, before)

    terms = compute(terms_kernel, (4, 128, 512), place, (gathered, *tokens))
    terms, theirs = lax.optimization_barrier((terms, theirs))
    mine_before, theirs_after = move(mine, next_engine), move(theirs, last_engine)
    mine_after, theirs_before = move(mine, last_engine), move(theirs, next_engine)
    terms = exchange(terms, "engine").astype(jnp.float32)
    kv_terms = jnp.sum(terms[:, :, 256:], axis=0)
    own = jnp.concatenate([terms[i, :, :128] for i in range(4)] + [kv_terms], axis=1)
    other = jnp.concatenate([terms[i, :, 128:256] for i in range(4)] + [kv_terms], axis=1)
    given = move(other.astype(jnp.bfloat16), other_core).astype(jnp.float32)
    own = (own + given).astype(jnp.bfloat16)
    squares = jnp.tile(split(squares), (1, 2))[:, :384]
    terms = jnp.stack(
        [
            jnp.concatenate(
                [
                    jnp.concatenate([own[:, i * 128 : (i + 1) * 128], own[:, 512:]], axis=1),
                    jnp.broadcast_to(squares, (8, 384)),
                ],
                axis=0,
            )
            for i in range(4)
        ]
    )
    terms, mine_before, mine_after, theirs_before, theirs_after = lax.optimization_barrier(
        (terms, mine_before, mine_after, theirs_before, theirs_after)
    )
    mine_across, theirs_across = move(mine_before, next_engine), move(theirs_after, last_engine)
    terms = exchange(terms, "tensor", ACROSS)
    total = jnp.sum(terms.astype(jnp.float32), axis=0)
    mean = (total[128, :128] + total[128, 128:256]) / 16384.0
    total = total[:128] * lax.rsqrt(mean + 1e-05)[:, None]

    places = positions[0]
    query = rotate(total[:, :128], places).astype(jnp.bfloat16)
    new_keys = rotate(total[:, 128:256], places).astype(jnp.bfloat16)
    new_values = total[:, 256:].astype(jnp.bfloat16)
    head_out = attend(query, new_keys, new_values, cache_keys[0], cache_values[0], offsets[0])

    head_out, mine_across, theirs_across = lax.optimization_barrier(
        (head_out, mine_across, theirs_across)
    )
    heads = jnp.concatenate([head_out, output_down_factor.T], axis=0)
    own = spread(heads, 4, "tensor", ACROSS)
    other = move(own, other_core)
    out_weights = (
        mine, theirs, mine_after, theirs_after, mine_across, theirs_across, mine_before, theirs_before
    )
    return compute(
        project_kernel, (128, 2048), place, (own, other, *out_weights), ((4, 512, 1152),)
    )


def solution(mesh):
    in_specs = (
        P(("engine", "fsdp"), "tensor"),
        P("tensor"),
        P(("engine", "fsdp"), "tensor"),
        P(("engine", "fsdp"), None),
        P(None, "tensor"),
        P("tensor", ("engine", "fsdp"), None),
        P(None, "tensor", ("engine", "fsdp")),
        P("tensor", None),
        P(None, "tensor", ("engine", "fsdp")),
        P(("engine", "fsdp"), None, None),
        P(("engine", "fsdp"), None, None),
        P(("engine", "fsdp"), None),
        P(("engine", "fsdp")),
    )
    out_specs = P(("engine", "fsdp"), "tensor")
    return jax.shard_map(
        per_device, mesh=mesh, in_specs=in_specs, out_specs=out_specs, check_vma=False
    )
```

```python
import jax
import jax.numpy as jnp
from jax import lax
from jax.experimental import pallas as pl
from jax.experimental.pallas import tpu as pltpu
from jax.sharding import PartitionSpec as P

AXES = ("engine", "fsdp", "tensor")


def turns(places):
    index = jnp.arange(64).astype(jnp.float32)
    inverse = jnp.exp(index * (-2.0 / 128) * jnp.log(jnp.float32(500000.0)))
    angle = places.astype(jnp.float32)[:, None] * inverse[None, :]
    cosine, sine = jnp.cos(angle), jnp.sin(angle)
    return jnp.concatenate([cosine, cosine], axis=1), jnp.concatenate([-sine, sine], axis=1)


def attend_kernel(
    offset_ref, terms_ref, cosine_ref, sine_ref, keys_ref, values_ref, down_ref, out_ref
):
    sums = terms_ref[0].astype(jnp.float32)
    for i in range(1, 4):
        sums = sums + terms_ref[i].astype(jnp.float32)
    mean = (sums[128:129, :128] + sums[128:129, 128:256]) / 16384.0
    scale = jnp.broadcast_to(lax.rsqrt(mean + 1e-05), (128, 128)).T
    query, new_keys, new_values = (sums[:128, i : i + 128] * scale for i in (0, 128, 256))
    cosine, sine = cosine_ref[...], sine_ref[...]
    query, new_keys = (
        (values * cosine + pltpu.roll(values, 64, 1) * sine).astype(jnp.bfloat16)
        for values in (query, new_keys)
    )
    inner = (((1,), (1,)), ((), ()))
    old = lax.dot_general(query, keys_ref[...], inner, preferred_element_type=jnp.float32)
    new = lax.dot_general(query, new_keys, inner, preferred_element_type=jnp.float32)
    old = jnp.where(
        lax.broadcasted_iota(jnp.int32, old.shape, 1) < offset_ref[0], old * 128**-0.5, -1e30
    )
    token = lax.broadcasted_iota(jnp.int32, new.shape, 0)
    new = jnp.where(
        lax.broadcasted_iota(jnp.int32, new.shape, 1) <= token, new * 128**-0.5, -1e30
    )
    top = jnp.maximum(jnp.max(old, axis=1, keepdims=True), jnp.max(new, axis=1, keepdims=True))
    old, new = jnp.exp(old - top), jnp.exp(new - top)
    whole = jnp.sum(old, axis=1, keepdims=True) + jnp.sum(new, axis=1, keepdims=True)
    out = jnp.dot(
        (old / whole).astype(jnp.bfloat16), values_ref[...], preferred_element_type=jnp.float32
    ) + jnp.dot(
        (new / whole).astype(jnp.bfloat16),
        new_values.astype(jnp.bfloat16),
        preferred_element_type=jnp.float32,
    )
    out_ref[:128] = out.astype(jnp.bfloat16)
    out_ref[128:] = down_ref[...]


ACROSS = [[0, 2, 4, 6], [1, 3, 5, 7]]
CORES = [[0, 1], [2, 3], [4, 5], [6, 7]]
ALONG_Z = [[2 * z + y for z in range(8)] for y in range(2)]


def shard_home(e, f, t):
    z, y = f // 2, f % 2
    home = z if t % 2 == z // 4 else 7 - z
    return t // 2, home * 2 + y, e * 2 + z // 4


def other_core(e, f, t):
    return e, f, t ^ 1


def other_y(e, f, t):
    return e, f ^ 1, t


def next_engine(e, f, t):
    return (e + 1) % 4, f, t


def last_engine(e, f, t):
    return (e + 3) % 4, f, t


def move(array, where):
    flat = lambda e, f, t: (e * 16 + f) * 8 + t
    pairs = [
        (flat(e, f, t), flat(*where(e, f, t)))
        for e in range(4)
        for f in range(16)
        for t in range(8)
    ]
    return lax.ppermute(array, AXES, pairs)


def exchange(array, axis, groups=None):
    return lax.all_to_all(
        array, axis, split_axis=0, concat_axis=0, tiled=True, axis_index_groups=groups
    )


def spread(array, count, axis, groups=None):
    return exchange(jnp.broadcast_to(array[None], (count, *array.shape)), axis, groups)


def split(sums):
    high = sums.astype(jnp.bfloat16)
    return jnp.concatenate([high, (sums - high.astype(jnp.float32)).astype(jnp.bfloat16)], axis=1)


def terms_kernel(place_ref, weight_ref, *refs):
    token_refs, out_ref = refs[:-1], refs[-1]
    engine, core = place_ref[0], place_ref[1]
    own = weight_ref[pl.ds(core * 8, 8), :256].reshape(2048, 128)
    other = weight_ref[pl.ds((1 - core) * 8, 8), :256].reshape(4, 512, 128)
    other = jnp.concatenate([other[3 - i] for i in range(4)], axis=0)
    query_weight = jnp.concatenate([own, other], axis=1)
    kv_weight = jnp.concatenate(
        [weight_ref[:, i : i + 32].reshape(512, 128) for i in (256, 288)], axis=1
    )
    some = pl.ds(pl.multiple_of(engine * 512, 512), 512)
    for ref, step, start in zip(token_refs, (0, 1, 2, 2, 3), (0, 0, 0, 64, 0), strict=True):
        rows = ref.shape[0]
        terms = jnp.concatenate(
            [
                jnp.dot(ref[...], query_weight, preferred_element_type=jnp.float32),
                jnp.dot(ref[:, some], kv_weight, preferred_element_type=jnp.float32),
            ],
            axis=1,
        )
        out_ref[lax.rem(engine + step, 4), start : start + rows] = terms.astype(jnp.bfloat16)


def project_kernel(place_ref, heads_ref, *refs):
    weight_refs, out_ref, weight_ref = refs[:8], refs[8], refs[9]
    engine, y = place_ref[0], place_ref[2]
    rows = jnp.concatenate([heads_ref[i] for i in range(8)], axis=1)
    heads, down = rows[:128], rows[128:]
    inner = (((1,), (1,)), ((), ()))
    mixed = lax.dot_general(heads, down, inner, preferred_element_type=jnp.float32)
    mixed = (2.0 * mixed).astype(jnp.bfloat16)
    heads = jnp.concatenate([heads, mixed, jnp.zeros_like(mixed)], axis=1)
    for step in range(4):
        for ref, half in zip(weight_refs[2 * step : 2 * step + 2], (y, 1 - y), strict=True):
            for z in range(8):
                at = pl.multiple_of(z * 64 + half * 32, 32)
                weight_ref[step, pl.ds(at, 32)] = ref[z * 32 : z * 32 + 32]
        out = lax.dot_general(
            heads, weight_ref[step], inner, preferred_element_type=jnp.float32
        )
        place = pl.multiple_of(lax.rem(engine + step, 4) * 512, 512)
        out_ref[:, pl.ds(place, 512)] = out.astype(jnp.bfloat16)


def compute(kernel, shape, place, arrays, scratch=()):
    return pl.pallas_call(
        kernel,
        out_shape=jax.ShapeDtypeStruct(shape, jnp.bfloat16),
        in_specs=[pl.BlockSpec(memory_space=pltpu.SMEM)]
        + [pl.BlockSpec(memory_space=pltpu.VMEM)] * len(arrays),
        out_specs=pl.BlockSpec(memory_space=pltpu.VMEM),
        scratch_shapes=[pltpu.VMEM(sizes, jnp.bfloat16) for sizes in scratch],
        compiler_params=pltpu.CompilerParams(vmem_limit_bytes=24 * 2**20),
    )(place, *arrays)


def per_device(
    layer_input,
    norm_gain,
    query_base,
    query_down,
    query_up,
    kv_base,
    output_base_weight,
    output_down_factor,
    output_up_factor,
    cache_keys,
    cache_values,
    positions,
    offsets,
):
    engine = lax.axis_index("engine")
    core = lax.axis_index("tensor") % 2
    place = jnp.stack([engine, core, lax.axis_index("fsdp") % 2]).astype(jnp.int32)

    merged_query = (
        query_base.astype(jnp.float32)
        + 2.0 * jnp.dot(query_down, query_up, preferred_element_type=jnp.float32)
    ).astype(jnp.bfloat16)
    out_shard = jnp.concatenate(
        [output_base_weight[:, 0, :].T, output_up_factor[:, 0, :].T, jnp.zeros((32, 64), jnp.bfloat16)],
        axis=1,
    )
    merged_query, out_shard = lax.optimization_barrier((merged_query, out_shard))
    query_shard = move(merged_query, shard_home)
    mine = spread(out_shard, 8, "fsdp", ALONG_Z).reshape(256, 1152)

    shard = jnp.concatenate([query_shard, kv_base[0, :, :128], kv_base[0, :, 128:]], axis=0)
    shards = jnp.broadcast_to(shard[None], (16, 320, 128))
    wide = layer_input.astype(jnp.float32)
    scaled = (wide * norm_gain.astype(jnp.float32)[None, :]).astype(jnp.bfloat16)
    before, after = move(scaled, next_engine), move(scaled, last_engine)
    shards, mine, before, after, layer_input = lax.optimization_barrier(
        (shards, mine, before, after, layer_input)
    )
    gathered = exchange(shards, "fsdp")

    wide = layer_input.astype(jnp.float32)
    squares = jnp.sum(wide * wide, axis=1)[None]
    squares = lax.all_gather(squares, "tensor", axis=0, tiled=True, axis_index_groups=CORES)
    squares = jnp.sum(squares, axis=0, keepdims=True)
    cosine, sine = turns(positions[0])
    squares, mine, before, after = lax.optimization_barrier((squares, mine, before, after))
    across_low, across_high = move(before[:64], next_engine), move(after[64:], last_engine)
    tokens = (scaled, after, across_low, across_high, before)
    theirs = move(mine, other_y)
    mine_before, mine_after = move(mine, next_engine), move(mine, last_engine)
    gathered, mine_before, mine_after = lax.optimization_barrier((gathered, mine_before, mine_after))
    mine_across = move(mine_before, next_engine)

    terms = compute(terms_kernel, (4, 128, 512), place, (gathered, *tokens))
    theirs_before, theirs_after = move(theirs, next_engine), move(theirs, last_engine)
    terms = exchange(terms, "engine").astype(jnp.float32)
    kv_terms = jnp.sum(terms[:, :, 256:], axis=0)
    own = jnp.concatenate([terms[i, :, :128] for i in range(4)] + [kv_terms], axis=1)
    other = jnp.concatenate([terms[i, :, 128:256] for i in range(4)] + [kv_terms], axis=1)
    given = move(other.astype(jnp.bfloat16), other_core).astype(jnp.float32)
    own = (own + given).astype(jnp.bfloat16)
    squares = jnp.tile(split(squares), (1, 2))[:, :384]
    terms = jnp.stack(
        [
            jnp.concatenate(
                [
                    jnp.concatenate([own[:, i * 128 : (i + 1) * 128], own[:, 512:]], axis=1),
                    jnp.broadcast_to(squares, (8, 384)),
                ],
                axis=0,
            )
            for i in range(4)
        ]
    )
    terms, mine_across, theirs_after, cosine, sine = lax.optimization_barrier(
        (terms, mine_across, theirs_after, cosine, sine)
    )
    theirs_across = move(theirs_after, last_engine)
    terms = exchange(terms, "tensor", ACROSS)
    heads = compute(
        attend_kernel,
        (192, 128),
        offsets,
        (terms, cosine, sine, cache_keys[0], cache_values[0], output_down_factor.T),
    )
    heads = lax.all_gather(heads[None], "tensor", axis=0, tiled=True)
    out_weights = (
        mine, theirs, mine_after, theirs_after, mine_across, theirs_across, mine_before, theirs_before
    )
    return compute(
        project_kernel, (128, 2048), place, (heads, *out_weights), ((4, 512, 1152),)
    )


def solution(mesh):
    in_specs = (
        P(("engine", "fsdp"), "tensor"),
        P("tensor"),
        P(("engine", "fsdp"), "tensor"),
        P(("engine", "fsdp"), None),
        P(None, "tensor"),
        P("tensor", ("engine", "fsdp"), None),
        P(None, "tensor", ("engine", "fsdp")),
        P("tensor", None),
        P(None, "tensor", ("engine", "fsdp")),
        P(("engine", "fsdp"), None, None),
        P(("engine", "fsdp"), None, None),
        P(("engine", "fsdp"), None),
        P(("engine", "fsdp")),
    )
    out_specs = P(("engine", "fsdp"), "tensor")
    return jax.shard_map(
        per_device, mesh=mesh, in_specs=in_specs, out_specs=out_specs, check_vma=False
    )
```

```python
import jax
import jax.numpy as jnp
from jax import lax
from jax.experimental import pallas as pl
from jax.experimental.pallas import tpu as pltpu
from jax.sharding import PartitionSpec as P

AXES = ("engine", "fsdp", "tensor")


def turns(places):
    index = jnp.arange(64).astype(jnp.float32)
    inverse = jnp.exp(index * (-2.0 / 128) * jnp.log(jnp.float32(500000.0)))
    angle = places.astype(jnp.float32)[:, None] * inverse[None, :]
    cosine, sine = jnp.cos(angle), jnp.sin(angle)
    return jnp.concatenate([cosine, cosine], axis=1), jnp.concatenate([-sine, sine], axis=1)


def attend_kernel(
    offset_ref, terms_ref, cosine_ref, sine_ref, keys_ref, values_ref, down_ref, out_ref
):
    sums = terms_ref[0].astype(jnp.float32)
    for i in range(1, 4):
        sums = sums + terms_ref[i].astype(jnp.float32)
    mean = (sums[128:129, :128] + sums[128:129, 128:256]) / 16384.0
    scale = jnp.broadcast_to(lax.rsqrt(mean + 1e-05), (128, 128)).T
    query, new_keys, new_values = (sums[:128, i : i + 128] * scale for i in (0, 128, 256))
    cosine, sine = cosine_ref[...], sine_ref[...]
    query, new_keys = (
        (values * cosine + pltpu.roll(values, 64, 1) * sine).astype(jnp.bfloat16)
        for values in (query, new_keys)
    )
    inner = (((1,), (1,)), ((), ()))
    old = lax.dot_general(query, keys_ref[...], inner, preferred_element_type=jnp.float32)
    new = lax.dot_general(query, new_keys, inner, preferred_element_type=jnp.float32)
    old = jnp.where(
        lax.broadcasted_iota(jnp.int32, old.shape, 1) < offset_ref[0], old * 128**-0.5, -1e30
    )
    token = lax.broadcasted_iota(jnp.int32, new.shape, 0)
    new = jnp.where(
        lax.broadcasted_iota(jnp.int32, new.shape, 1) <= token, new * 128**-0.5, -1e30
    )
    top = jnp.maximum(jnp.max(old, axis=1, keepdims=True), jnp.max(new, axis=1, keepdims=True))
    old, new = jnp.exp(old - top), jnp.exp(new - top)
    whole = jnp.sum(old, axis=1, keepdims=True) + jnp.sum(new, axis=1, keepdims=True)
    out = jnp.dot(
        (old / whole).astype(jnp.bfloat16), values_ref[...], preferred_element_type=jnp.float32
    ) + jnp.dot(
        (new / whole).astype(jnp.bfloat16),
        new_values.astype(jnp.bfloat16),
        preferred_element_type=jnp.float32,
    )
    out_ref[:128] = out.astype(jnp.bfloat16)
    out_ref[128:] = down_ref[...]


ACROSS = [[0, 2, 4, 6], [1, 3, 5, 7]]
CORES = [[0, 1], [2, 3], [4, 5], [6, 7]]
ALONG_Z = [[2 * z + y for z in range(8)] for y in range(2)]


def shard_home(e, f, t):
    z, y = f // 2, f % 2
    home = z if t % 2 == z // 4 else 7 - z
    return t // 2, home * 2 + y, e * 2 + z // 4


def other_core(e, f, t):
    return e, f, t ^ 1


def other_y(e, f, t):
    return e, f ^ 1, t


def next_engine(e, f, t):
    return (e + 1) % 4, f, t


def last_engine(e, f, t):
    return (e + 3) % 4, f, t


def move(array, where):
    flat = lambda e, f, t: (e * 16 + f) * 8 + t
    pairs = [
        (flat(e, f, t), flat(*where(e, f, t)))
        for e in range(4)
        for f in range(16)
        for t in range(8)
    ]
    return lax.ppermute(array, AXES, pairs)


def exchange(array, axis, groups=None):
    return lax.all_to_all(
        array, axis, split_axis=0, concat_axis=0, tiled=True, axis_index_groups=groups
    )


def spread(array, count, axis, groups=None):
    return exchange(jnp.broadcast_to(array[None], (count, *array.shape)), axis, groups)


def split(sums):
    high = sums.astype(jnp.bfloat16)
    return jnp.concatenate([high, (sums - high.astype(jnp.float32)).astype(jnp.bfloat16)], axis=1)


def terms_kernel(place_ref, weight_ref, *refs):
    token_refs, out_ref = refs[:-1], refs[-1]
    engine, core = place_ref[0], place_ref[1]
    own = weight_ref[pl.ds(core * 8, 8), :256].reshape(2048, 128)
    other = weight_ref[pl.ds((1 - core) * 8, 8), :256].reshape(4, 512, 128)
    other = jnp.concatenate([other[3 - i] for i in range(4)], axis=0)
    query_weight = jnp.concatenate([own, other], axis=1)
    kv_weight = jnp.concatenate(
        [weight_ref[:, i : i + 32].reshape(512, 128) for i in (256, 288)], axis=1
    )
    some = pl.ds(pl.multiple_of(engine * 512, 512), 512)
    for ref, step, start in zip(token_refs, (0, 1, 2, 2, 3), (0, 0, 0, 64, 0), strict=True):
        rows = ref.shape[0]
        terms = jnp.concatenate(
            [
                jnp.dot(ref[...], query_weight, preferred_element_type=jnp.float32),
                jnp.dot(ref[:, some], kv_weight, preferred_element_type=jnp.float32),
            ],
            axis=1,
        )
        out_ref[lax.rem(engine + step, 4), start : start + rows] = terms.astype(jnp.bfloat16)


def project_kernel(place_ref, heads_ref, *refs):
    weight_refs, out_ref, weight_ref = refs[:8], refs[8], refs[9]
    engine, y = place_ref[0], place_ref[2]
    rows = jnp.concatenate([heads_ref[i] for i in range(8)], axis=1)
    heads, down = rows[:128], rows[128:]
    inner = (((1,), (1,)), ((), ()))
    mixed = lax.dot_general(heads, down, inner, preferred_element_type=jnp.float32)
    mixed = (2.0 * mixed).astype(jnp.bfloat16)
    heads = jnp.concatenate([heads, mixed, jnp.zeros_like(mixed)], axis=1)
    for step in range(4):
        for ref, half in zip(weight_refs[2 * step : 2 * step + 2], (y, 1 - y), strict=True):
            for z in range(8):
                at = pl.multiple_of(z * 64 + half * 32, 32)
                weight_ref[step, pl.ds(at, 32)] = ref[z * 32 : z * 32 + 32]
        out = lax.dot_general(
            heads, weight_ref[step], inner, preferred_element_type=jnp.float32
        )
        place = pl.multiple_of(lax.rem(engine + step, 4) * 512, 512)
        out_ref[:, pl.ds(place, 512)] = out.astype(jnp.bfloat16)


def compute(kernel, shape, place, arrays, scratch=()):
    return pl.pallas_call(
        kernel,
        out_shape=jax.ShapeDtypeStruct(shape, jnp.bfloat16),
        in_specs=[pl.BlockSpec(memory_space=pltpu.SMEM)]
        + [pl.BlockSpec(memory_space=pltpu.VMEM)] * len(arrays),
        out_specs=pl.BlockSpec(memory_space=pltpu.VMEM),
        scratch_shapes=[pltpu.VMEM(sizes, jnp.bfloat16) for sizes in scratch],
        compiler_params=pltpu.CompilerParams(vmem_limit_bytes=24 * 2**20),
    )(place, *arrays)


def per_device(
    layer_input,
    norm_gain,
    query_base,
    query_down,
    query_up,
    kv_base,
    output_base_weight,
    output_down_factor,
    output_up_factor,
    cache_keys,
    cache_values,
    positions,
    offsets,
):
    engine = lax.axis_index("engine")
    core = lax.axis_index("tensor") % 2
    place = jnp.stack([engine, core, lax.axis_index("fsdp") % 2]).astype(jnp.int32)

    merged_query = (
        query_base.astype(jnp.float32)
        + 2.0 * jnp.dot(query_down, query_up, preferred_element_type=jnp.float32)
    ).astype(jnp.bfloat16)
    out_shard = jnp.concatenate(
        [output_base_weight[:, 0, :].T, output_up_factor[:, 0, :].T, jnp.zeros((32, 64), jnp.bfloat16)],
        axis=1,
    )
    merged_query, out_shard = lax.optimization_barrier((merged_query, out_shard))
    query_shard = move(merged_query, shard_home)
    mine = spread(out_shard, 8, "fsdp", ALONG_Z).reshape(256, 1152)

    shard = jnp.concatenate([query_shard, kv_base[0, :, :128], kv_base[0, :, 128:]], axis=0)
    shards = jnp.broadcast_to(shard[None], (16, 320, 128))
    wide = layer_input.astype(jnp.float32)
    scaled = (wide * norm_gain.astype(jnp.float32)[None, :]).astype(jnp.bfloat16)
    before, after = move(scaled, next_engine), move(scaled, last_engine)
    shards, mine, before, after, layer_input = lax.optimization_barrier(
        (shards, mine, before, after, layer_input)
    )
    gathered = exchange(shards, "fsdp")

    wide = layer_input.astype(jnp.float32)
    squares = jnp.sum(wide * wide, axis=1)[None]
    squares = lax.all_gather(squares, "tensor", axis=0, tiled=True, axis_index_groups=CORES)
    squares = jnp.sum(squares, axis=0, keepdims=True)
    cosine, sine = turns(positions[0])
    squares, mine, before, after = lax.optimization_barrier((squares, mine, before, after))
    across_low, across_high = move(before[:64], next_engine), move(after[64:], last_engine)
    tokens = (scaled, after, across_low, across_high, before)
    theirs = move(mine, other_y)
    mine_before, mine_after = move(mine, next_engine), move(mine, last_engine)

    terms = compute(terms_kernel, (4, 128, 512), place, (gathered, *tokens))
    theirs_before, theirs_after = move(theirs, next_engine), move(theirs, last_engine)
    terms = exchange(terms, "engine").astype(jnp.float32)
    kv_terms = jnp.sum(terms[:, :, 256:], axis=0)
    own = jnp.concatenate([terms[i, :, :128] for i in range(4)] + [kv_terms], axis=1)
    other = jnp.concatenate([terms[i, :, 128:256] for i in range(4)] + [kv_terms], axis=1)
    given = move(other.astype(jnp.bfloat16), other_core).astype(jnp.float32)
    own = (own + given).astype(jnp.bfloat16)
    squares = jnp.tile(split(squares), (1, 2))[:, :384]
    terms = jnp.stack(
        [
            jnp.concatenate(
                [
                    jnp.concatenate([own[:, i * 128 : (i + 1) * 128], own[:, 512:]], axis=1),
                    jnp.broadcast_to(squares, (8, 384)),
                ],
                axis=0,
            )
            for i in range(4)
        ]
    )
    terms, mine_before, mine_after, theirs_after, cosine, sine = lax.optimization_barrier(
        (terms, mine_before, mine_after, theirs_after, cosine, sine)
    )
    theirs_across = move(theirs_after, last_engine)
    mine_across = move(mine_before, next_engine)
    terms = exchange(terms, "tensor", ACROSS)
    heads = compute(
        attend_kernel,
        (192, 128),
        offsets,
        (terms, cosine, sine, cache_keys[0], cache_values[0], output_down_factor.T),
    )
    heads = lax.all_gather(heads[None], "tensor", axis=0, tiled=True)
    out_weights = (
        mine, theirs, mine_after, theirs_after, mine_across, theirs_across, mine_before, theirs_before
    )
    return compute(
        project_kernel, (128, 2048), place, (heads, *out_weights), ((4, 512, 1152),)
    )


def solution(mesh):
    in_specs = (
        P(("engine", "fsdp"), "tensor"),
        P("tensor"),
        P(("engine", "fsdp"), "tensor"),
        P(("engine", "fsdp"), None),
        P(None, "tensor"),
        P("tensor", ("engine", "fsdp"), None),
        P(None, "tensor", ("engine", "fsdp")),
        P("tensor", None),
        P(None, "tensor", ("engine", "fsdp")),
        P(("engine", "fsdp"), None, None),
        P(("engine", "fsdp"), None, None),
        P(("engine", "fsdp"), None),
        P(("engine", "fsdp")),
    )
    out_specs = P(("engine", "fsdp"), "tensor")
    return jax.shard_map(
        per_device, mesh=mesh, in_specs=in_specs, out_specs=out_specs, check_vma=False
    )
```

```python
import jax
import jax.numpy as jnp
from jax import lax
from jax.experimental import pallas as pl
from jax.experimental.pallas import tpu as pltpu
from jax.sharding import PartitionSpec as P

AXES = ("engine", "fsdp", "tensor")


def turns(places):
    index = jnp.arange(64).astype(jnp.float32)
    inverse = jnp.exp(index * (-2.0 / 128) * jnp.log(jnp.float32(500000.0)))
    angle = places.astype(jnp.float32)[:, None] * inverse[None, :]
    cosine, sine = jnp.cos(angle), jnp.sin(angle)
    return jnp.concatenate([cosine, cosine], axis=1), jnp.concatenate([-sine, sine], axis=1)


def attend_kernel(
    offset_ref, terms_ref, cosine_ref, sine_ref, keys_ref, values_ref, down_ref, out_ref
):
    sums = terms_ref[0].astype(jnp.float32)
    for i in range(1, 4):
        sums = sums + terms_ref[i].astype(jnp.float32)
    mean = (sums[128:129, :128] + sums[128:129, 128:256]) / 16384.0
    scale = jnp.broadcast_to(lax.rsqrt(mean + 1e-05), (128, 128)).T
    query, new_keys, new_values = (sums[:128, i : i + 128] * scale for i in (0, 128, 256))
    cosine, sine = cosine_ref[...], sine_ref[...]
    query, new_keys = (
        (values * cosine + pltpu.roll(values, 64, 1) * sine).astype(jnp.bfloat16)
        for values in (query, new_keys)
    )
    inner = (((1,), (1,)), ((), ()))
    old = lax.dot_general(query, keys_ref[...], inner, preferred_element_type=jnp.float32)
    new = lax.dot_general(query, new_keys, inner, preferred_element_type=jnp.float32)
    old = jnp.where(
        lax.broadcasted_iota(jnp.int32, old.shape, 1) < offset_ref[0], old * 128**-0.5, -1e30
    )
    token = lax.broadcasted_iota(jnp.int32, new.shape, 0)
    new = jnp.where(
        lax.broadcasted_iota(jnp.int32, new.shape, 1) <= token, new * 128**-0.5, -1e30
    )
    top = jnp.maximum(jnp.max(old, axis=1, keepdims=True), jnp.max(new, axis=1, keepdims=True))
    old, new = jnp.exp(old - top), jnp.exp(new - top)
    whole = jnp.sum(old, axis=1, keepdims=True) + jnp.sum(new, axis=1, keepdims=True)
    out = jnp.dot(
        (old / whole).astype(jnp.bfloat16), values_ref[...], preferred_element_type=jnp.float32
    ) + jnp.dot(
        (new / whole).astype(jnp.bfloat16),
        new_values.astype(jnp.bfloat16),
        preferred_element_type=jnp.float32,
    )
    out_ref[:128] = out.astype(jnp.bfloat16)
    out_ref[128:] = down_ref[...]


ACROSS = [[0, 2, 4, 6], [1, 3, 5, 7]]
CORES = [[0, 1], [2, 3], [4, 5], [6, 7]]
ALONG_Z = [[2 * z + y for z in range(8)] for y in range(2)]


def shard_home(e, f, t):
    z, y = f // 2, f % 2
    home = z if t % 2 == z // 4 else 7 - z
    return t // 2, home * 2 + y, e * 2 + z // 4


def other_core(e, f, t):
    return e, f, t ^ 1


def other_y(e, f, t):
    return e, f ^ 1, t


def next_engine(e, f, t):
    return (e + 1) % 4, f, t


def last_engine(e, f, t):
    return (e + 3) % 4, f, t


def move(array, where):
    flat = lambda e, f, t: (e * 16 + f) * 8 + t
    pairs = [
        (flat(e, f, t), flat(*where(e, f, t)))
        for e in range(4)
        for f in range(16)
        for t in range(8)
    ]
    return lax.ppermute(array, AXES, pairs)


def exchange(array, axis, groups=None):
    return lax.all_to_all(
        array, axis, split_axis=0, concat_axis=0, tiled=True, axis_index_groups=groups
    )


def spread(array, count, axis, groups=None):
    return exchange(jnp.broadcast_to(array[None], (count, *array.shape)), axis, groups)


def split(sums):
    high = sums.astype(jnp.bfloat16)
    return jnp.concatenate([high, (sums - high.astype(jnp.float32)).astype(jnp.bfloat16)], axis=1)


def terms_kernel(place_ref, weight_ref, *refs):
    token_refs, out_ref = refs[:-1], refs[-1]
    engine, core = place_ref[0], place_ref[1]
    own = weight_ref[pl.ds(core * 8, 8), :256].reshape(2048, 128)
    other = weight_ref[pl.ds((1 - core) * 8, 8), :256].reshape(4, 512, 128)
    other = jnp.concatenate([other[3 - i] for i in range(4)], axis=0)
    query_weight = jnp.concatenate([own, other], axis=1)
    kv_weight = jnp.concatenate(
        [weight_ref[:, i : i + 32].reshape(512, 128) for i in (256, 288)], axis=1
    )
    some = pl.ds(pl.multiple_of(engine * 512, 512), 512)
    tokens = jnp.concatenate([ref[...] for ref in token_refs], axis=0)
    some_tokens = jnp.concatenate([ref[:, some] for ref in token_refs], axis=0)
    terms = jnp.concatenate(
        [
            jnp.dot(tokens, query_weight, preferred_element_type=jnp.float32),
            jnp.dot(some_tokens, kv_weight, preferred_element_type=jnp.float32),
        ],
        axis=1,
    ).astype(jnp.bfloat16)
    for step in range(4):
        out_ref[lax.rem(engine + step, 4)] = terms[step * 128 : step * 128 + 128]


def project_kernel(place_ref, heads_ref, *refs):
    weight_refs, out_ref, weight_ref = refs[:8], refs[8], refs[9]
    engine, y = place_ref[0], place_ref[2]
    rows = jnp.concatenate([heads_ref[i] for i in range(8)], axis=1)
    heads, down = rows[:128], rows[128:]
    inner = (((1,), (1,)), ((), ()))
    mixed = lax.dot_general(heads, down, inner, preferred_element_type=jnp.float32)
    mixed = (2.0 * mixed).astype(jnp.bfloat16)
    heads = jnp.concatenate([heads, mixed, jnp.zeros_like(mixed)], axis=1)
    for step in range(4):
        for ref, half in zip(weight_refs[2 * step : 2 * step + 2], (y, 1 - y), strict=True):
            for z in range(8):
                at = pl.multiple_of(z * 64 + half * 32, 32)
                weight_ref[step, pl.ds(at, 32)] = ref[z * 32 : z * 32 + 32]
        out = lax.dot_general(
            heads, weight_ref[step], inner, preferred_element_type=jnp.float32
        )
        place = pl.multiple_of(lax.rem(engine + step, 4) * 512, 512)
        out_ref[:, pl.ds(place, 512)] = out.astype(jnp.bfloat16)


def compute(kernel, shape, place, arrays, scratch=()):
    return pl.pallas_call(
        kernel,
        out_shape=jax.ShapeDtypeStruct(shape, jnp.bfloat16),
        in_specs=[pl.BlockSpec(memory_space=pltpu.SMEM)]
        + [pl.BlockSpec(memory_space=pltpu.VMEM)] * len(arrays),
        out_specs=pl.BlockSpec(memory_space=pltpu.VMEM),
        scratch_shapes=[pltpu.VMEM(sizes, jnp.bfloat16) for sizes in scratch],
        compiler_params=pltpu.CompilerParams(vmem_limit_bytes=24 * 2**20),
    )(place, *arrays)


def per_device(
    layer_input,
    norm_gain,
    query_base,
    query_down,
    query_up,
    kv_base,
    output_base_weight,
    output_down_factor,
    output_up_factor,
    cache_keys,
    cache_values,
    positions,
    offsets,
):
    engine = lax.axis_index("engine")
    core = lax.axis_index("tensor") % 2
    place = jnp.stack([engine, core, lax.axis_index("fsdp") % 2]).astype(jnp.int32)

    merged_query = (
        query_base.astype(jnp.float32)
        + 2.0 * jnp.dot(query_down, query_up, preferred_element_type=jnp.float32)
    ).astype(jnp.bfloat16)
    out_shard = jnp.concatenate(
        [output_base_weight[:, 0, :].T, output_up_factor[:, 0, :].T, jnp.zeros((32, 64), jnp.bfloat16)],
        axis=1,
    )
    merged_query, out_shard = lax.optimization_barrier((merged_query, out_shard))
    query_shard = move(merged_query, shard_home)
    mine = spread(out_shard, 8, "fsdp", ALONG_Z).reshape(256, 1152)

    shard = jnp.concatenate([query_shard, kv_base[0, :, :128], kv_base[0, :, 128:]], axis=0)
    shards = jnp.broadcast_to(shard[None], (16, 320, 128))
    wide = layer_input.astype(jnp.float32)
    scaled = (wide * norm_gain.astype(jnp.float32)[None, :]).astype(jnp.bfloat16)
    before, after = move(scaled, next_engine), move(scaled, last_engine)
    shards, mine, before, after, layer_input = lax.optimization_barrier(
        (shards, mine, before, after, layer_input)
    )
    gathered = exchange(shards, "fsdp")

    wide = layer_input.astype(jnp.float32)
    squares = jnp.sum(wide * wide, axis=1)[None]
    squares = lax.all_gather(squares, "tensor", axis=0, tiled=True, axis_index_groups=CORES)
    squares = jnp.sum(squares, axis=0, keepdims=True)
    cosine, sine = turns(positions[0])
    squares, mine, before, after = lax.optimization_barrier((squares, mine, before, after))
    across_low, across_high = move(before[:64], next_engine), move(after[64:], last_engine)
    tokens = (scaled, after, across_low, across_high, before)
    theirs = move(mine, other_y)
    mine_before, mine_after = move(mine, next_engine), move(mine, last_engine)

    terms = compute(terms_kernel, (4, 128, 512), place, (gathered, *tokens))
    theirs_before, theirs_after = move(theirs, next_engine), move(theirs, last_engine)
    terms = exchange(terms, "engine").astype(jnp.float32)
    kv_terms = jnp.sum(terms[:, :, 256:], axis=0)
    own = jnp.concatenate([terms[i, :, :128] for i in range(4)] + [kv_terms], axis=1)
    other = jnp.concatenate([terms[i, :, 128:256] for i in range(4)] + [kv_terms], axis=1)
    given = move(other.astype(jnp.bfloat16), other_core).astype(jnp.float32)
    own = (own + given).astype(jnp.bfloat16)
    squares = jnp.tile(split(squares), (1, 2))[:, :384]
    terms = jnp.stack(
        [
            jnp.concatenate(
                [
                    jnp.concatenate([own[:, i * 128 : (i + 1) * 128], own[:, 512:]], axis=1),
                    jnp.broadcast_to(squares, (8, 384)),
                ],
                axis=0,
            )
            for i in range(4)
        ]
    )
    terms, mine_before, mine_after, theirs_after, cosine, sine = lax.optimization_barrier(
        (terms, mine_before, mine_after, theirs_after, cosine, sine)
    )
    theirs_across = move(theirs_after, last_engine)
    mine_across = move(mine_before, next_engine)
    terms = exchange(terms, "tensor", ACROSS)
    heads = compute(
        attend_kernel,
        (192, 128),
        offsets,
        (terms, cosine, sine, cache_keys[0], cache_values[0], output_down_factor.T),
    )
    heads = lax.all_gather(heads[None], "tensor", axis=0, tiled=True)
    out_weights = (
        mine, theirs, mine_after, theirs_after, mine_across, theirs_across, mine_before, theirs_before
    )
    return compute(
        project_kernel, (128, 2048), place, (heads, *out_weights), ((4, 512, 1152),)
    )


def solution(mesh):
    in_specs = (
        P(("engine", "fsdp"), "tensor"),
        P("tensor"),
        P(("engine", "fsdp"), "tensor"),
        P(("engine", "fsdp"), None),
        P(None, "tensor"),
        P("tensor", ("engine", "fsdp"), None),
        P(None, "tensor", ("engine", "fsdp")),
        P("tensor", None),
        P(None, "tensor", ("engine", "fsdp")),
        P(("engine", "fsdp"), None, None),
        P(("engine", "fsdp"), None, None),
        P(("engine", "fsdp"), None),
        P(("engine", "fsdp")),
    )
    out_specs = P(("engine", "fsdp"), "tensor")
    return jax.shard_map(
        per_device, mesh=mesh, in_specs=in_specs, out_specs=out_specs, check_vma=False
    )
```

```python
import jax
import jax.numpy as jnp
from jax import lax
from jax.experimental import pallas as pl
from jax.experimental.pallas import tpu as pltpu
from jax.sharding import PartitionSpec as P

AXES = ("engine", "fsdp", "tensor")


def turns(places):
    index = jnp.arange(64).astype(jnp.float32)
    inverse = jnp.exp(index * (-2.0 / 128) * jnp.log(jnp.float32(500000.0)))
    angle = places.astype(jnp.float32)[:, None] * inverse[None, :]
    cosine, sine = jnp.cos(angle), jnp.sin(angle)
    return jnp.concatenate([cosine, cosine], axis=1), jnp.concatenate([-sine, sine], axis=1)


def attend_kernel(
    offset_ref, terms_ref, cosine_ref, sine_ref, keys_ref, values_ref, down_ref, out_ref
):
    sums = terms_ref[0].astype(jnp.float32)
    for i in range(1, 4):
        sums = sums + terms_ref[i].astype(jnp.float32)
    mean = (sums[128:129, :128] + sums[128:129, 128:256]) / 16384.0
    scale = jnp.broadcast_to(lax.rsqrt(mean + 1e-05), (128, 128)).T
    query, new_keys, new_values = (sums[:128, i : i + 128] * scale for i in (0, 128, 256))
    cosine, sine = cosine_ref[...], sine_ref[...]
    query, new_keys = (
        (values * cosine + pltpu.roll(values, 64, 1) * sine).astype(jnp.bfloat16)
        for values in (query, new_keys)
    )
    inner = (((1,), (1,)), ((), ()))
    old = lax.dot_general(query, keys_ref[...], inner, preferred_element_type=jnp.float32)
    new = lax.dot_general(query, new_keys, inner, preferred_element_type=jnp.float32)
    old = jnp.where(
        lax.broadcasted_iota(jnp.int32, old.shape, 1) < offset_ref[0], old * 128**-0.5, -1e30
    )
    token = lax.broadcasted_iota(jnp.int32, new.shape, 0)
    new = jnp.where(
        lax.broadcasted_iota(jnp.int32, new.shape, 1) <= token, new * 128**-0.5, -1e30
    )
    top = jnp.maximum(jnp.max(old, axis=1, keepdims=True), jnp.max(new, axis=1, keepdims=True))
    old, new = jnp.exp(old - top), jnp.exp(new - top)
    whole = jnp.sum(old, axis=1, keepdims=True) + jnp.sum(new, axis=1, keepdims=True)
    out = jnp.dot(
        (old / whole).astype(jnp.bfloat16), values_ref[...], preferred_element_type=jnp.float32
    ) + jnp.dot(
        (new / whole).astype(jnp.bfloat16),
        new_values.astype(jnp.bfloat16),
        preferred_element_type=jnp.float32,
    )
    out_ref[:128] = out.astype(jnp.bfloat16)
    out_ref[128:] = down_ref[...]


ACROSS = [[0, 2, 4, 6], [1, 3, 5, 7]]
CORES = [[0, 1], [2, 3], [4, 5], [6, 7]]
ALONG_Z = [[2 * z + y for z in range(8)] for y in range(2)]


def shard_home(e, f, t):
    z, y = f // 2, f % 2
    home = z if t % 2 == z // 4 else 7 - z
    return t // 2, home * 2 + y, e * 2 + z // 4


def other_core(e, f, t):
    return e, f, t ^ 1


def other_y(e, f, t):
    return e, f ^ 1, t


def next_engine(e, f, t):
    return (e + 1) % 4, f, t


def last_engine(e, f, t):
    return (e + 3) % 4, f, t


def move(array, where):
    flat = lambda e, f, t: (e * 16 + f) * 8 + t
    pairs = [
        (flat(e, f, t), flat(*where(e, f, t)))
        for e in range(4)
        for f in range(16)
        for t in range(8)
    ]
    return lax.ppermute(array, AXES, pairs)


def exchange(array, axis, groups=None):
    return lax.all_to_all(
        array, axis, split_axis=0, concat_axis=0, tiled=True, axis_index_groups=groups
    )


def spread(array, count, axis, groups=None):
    return exchange(jnp.broadcast_to(array[None], (count, *array.shape)), axis, groups)


def split(sums):
    high = sums.astype(jnp.bfloat16)
    return jnp.concatenate([high, (sums - high.astype(jnp.float32)).astype(jnp.bfloat16)], axis=1)


def terms_kernel(place_ref, weight_ref, *refs):
    token_refs, out_ref = refs[:-1], refs[-1]
    engine, core = place_ref[0], place_ref[1]
    own = weight_ref[pl.ds(core * 8, 8), :256].reshape(2048, 128)
    other = weight_ref[pl.ds((1 - core) * 8, 8), :256].reshape(4, 512, 128)
    other = jnp.concatenate([other[3 - i] for i in range(4)], axis=0)
    query_weight = jnp.concatenate([own, other], axis=1)
    kv_weight = jnp.concatenate(
        [weight_ref[:, i : i + 32].reshape(512, 128) for i in (256, 288)], axis=1
    )
    some = pl.ds(pl.multiple_of(engine * 512, 512), 512)
    tokens = jnp.concatenate([ref[...] for ref in token_refs], axis=0)
    some_tokens = jnp.concatenate([ref[:, some] for ref in token_refs], axis=0)
    terms = jnp.concatenate(
        [
            jnp.dot(tokens, query_weight, preferred_element_type=jnp.float32),
            jnp.dot(some_tokens, kv_weight, preferred_element_type=jnp.float32),
        ],
        axis=1,
    ).astype(jnp.bfloat16)
    for step in range(4):
        out_ref[lax.rem(engine + step, 4)] = terms[step * 128 : step * 128 + 128]


def project_kernel(place_ref, heads_ref, *refs):
    weight_refs, out_ref, weight_ref = refs[:8], refs[8], refs[9]
    engine, y = place_ref[0], place_ref[2]
    rows = jnp.concatenate([heads_ref[i] for i in range(8)], axis=1)
    heads, down = rows[:128], rows[128:]
    inner = (((1,), (1,)), ((), ()))
    mixed = lax.dot_general(heads, down, inner, preferred_element_type=jnp.float32)
    mixed = (2.0 * mixed).astype(jnp.bfloat16)
    heads = jnp.concatenate([heads, mixed, jnp.zeros_like(mixed)], axis=1)
    for step in range(4):
        for ref, half in zip(weight_refs[2 * step : 2 * step + 2], (y, 1 - y), strict=True):
            for z in range(8):
                at = pl.multiple_of(z * 64 + half * 32, 32)
                weight_ref[step, pl.ds(at, 32)] = ref[z * 32 : z * 32 + 32]
    out = lax.dot_general(
        heads, weight_ref[...].reshape(2048, 1152), inner, preferred_element_type=jnp.float32
    ).astype(jnp.bfloat16)
    for step in range(4):
        place = pl.multiple_of(lax.rem(engine + step, 4) * 512, 512)
        out_ref[:, pl.ds(place, 512)] = out[:, step * 512 : step * 512 + 512]


def compute(kernel, shape, place, arrays, scratch=()):
    return pl.pallas_call(
        kernel,
        out_shape=jax.ShapeDtypeStruct(shape, jnp.bfloat16),
        in_specs=[pl.BlockSpec(memory_space=pltpu.SMEM)]
        + [pl.BlockSpec(memory_space=pltpu.VMEM)] * len(arrays),
        out_specs=pl.BlockSpec(memory_space=pltpu.VMEM),
        scratch_shapes=[pltpu.VMEM(sizes, jnp.bfloat16) for sizes in scratch],
        compiler_params=pltpu.CompilerParams(vmem_limit_bytes=24 * 2**20),
    )(place, *arrays)


def per_device(
    layer_input,
    norm_gain,
    query_base,
    query_down,
    query_up,
    kv_base,
    output_base_weight,
    output_down_factor,
    output_up_factor,
    cache_keys,
    cache_values,
    positions,
    offsets,
):
    engine = lax.axis_index("engine")
    core = lax.axis_index("tensor") % 2
    place = jnp.stack([engine, core, lax.axis_index("fsdp") % 2]).astype(jnp.int32)

    merged_query = (
        query_base.astype(jnp.float32)
        + 2.0 * jnp.dot(query_down, query_up, preferred_element_type=jnp.float32)
    ).astype(jnp.bfloat16)
    out_shard = jnp.concatenate(
        [output_base_weight[:, 0, :].T, output_up_factor[:, 0, :].T, jnp.zeros((32, 64), jnp.bfloat16)],
        axis=1,
    )
    merged_query, out_shard = lax.optimization_barrier((merged_query, out_shard))
    query_shard = move(merged_query, shard_home)
    mine = spread(out_shard, 8, "fsdp", ALONG_Z).reshape(256, 1152)

    shard = jnp.concatenate([query_shard, kv_base[0, :, :128], kv_base[0, :, 128:]], axis=0)
    shards = jnp.broadcast_to(shard[None], (16, 320, 128))
    wide = layer_input.astype(jnp.float32)
    scaled = (wide * norm_gain.astype(jnp.float32)[None, :]).astype(jnp.bfloat16)
    before, after = move(scaled, next_engine), move(scaled, last_engine)
    shards, mine, before, after, layer_input = lax.optimization_barrier(
        (shards, mine, before, after, layer_input)
    )
    gathered = exchange(shards, "fsdp")

    wide = layer_input.astype(jnp.float32)
    squares = jnp.sum(wide * wide, axis=1)[None]
    squares = lax.all_gather(squares, "tensor", axis=0, tiled=True, axis_index_groups=CORES)
    squares = jnp.sum(squares, axis=0, keepdims=True)
    cosine, sine = turns(positions[0])
    squares, mine, before, after = lax.optimization_barrier((squares, mine, before, after))
    across_low, across_high = move(before[:64], next_engine), move(after[64:], last_engine)
    tokens = (scaled, after, across_low, across_high, before)
    theirs = move(mine, other_y)
    mine_before, mine_after = move(mine, next_engine), move(mine, last_engine)

    terms = compute(terms_kernel, (4, 128, 512), place, (gathered, *tokens))
    theirs_before, theirs_after = move(theirs, next_engine), move(theirs, last_engine)
    terms = exchange(terms, "engine").astype(jnp.float32)
    kv_terms = jnp.sum(terms[:, :, 256:], axis=0)
    own = jnp.concatenate([terms[i, :, :128] for i in range(4)] + [kv_terms], axis=1)
    other = jnp.concatenate([terms[i, :, 128:256] for i in range(4)] + [kv_terms], axis=1)
    given = move(other.astype(jnp.bfloat16), other_core).astype(jnp.float32)
    own = (own + given).astype(jnp.bfloat16)
    squares = jnp.tile(split(squares), (1, 2))[:, :384]
    terms = jnp.stack(
        [
            jnp.concatenate(
                [
                    jnp.concatenate([own[:, i * 128 : (i + 1) * 128], own[:, 512:]], axis=1),
                    jnp.broadcast_to(squares, (8, 384)),
                ],
                axis=0,
            )
            for i in range(4)
        ]
    )
    terms, mine_before, mine_after, theirs_after, cosine, sine = lax.optimization_barrier(
        (terms, mine_before, mine_after, theirs_after, cosine, sine)
    )
    theirs_across = move(theirs_after, last_engine)
    mine_across = move(mine_before, next_engine)
    terms = exchange(terms, "tensor", ACROSS)
    heads = compute(
        attend_kernel,
        (192, 128),
        offsets,
        (terms, cosine, sine, cache_keys[0], cache_values[0], output_down_factor.T),
    )
    heads = lax.all_gather(heads[None], "tensor", axis=0, tiled=True)
    out_weights = (
        mine, theirs, mine_after, theirs_after, mine_across, theirs_across, mine_before, theirs_before
    )
    return compute(
        project_kernel, (128, 2048), place, (heads, *out_weights), ((4, 512, 1152),)
    )


def solution(mesh):
    in_specs = (
        P(("engine", "fsdp"), "tensor"),
        P("tensor"),
        P(("engine", "fsdp"), "tensor"),
        P(("engine", "fsdp"), None),
        P(None, "tensor"),
        P("tensor", ("engine", "fsdp"), None),
        P(None, "tensor", ("engine", "fsdp")),
        P("tensor", None),
        P(None, "tensor", ("engine", "fsdp")),
        P(("engine", "fsdp"), None, None),
        P(("engine", "fsdp"), None, None),
        P(("engine", "fsdp"), None),
        P(("engine", "fsdp")),
    )
    out_specs = P(("engine", "fsdp"), "tensor")
    return jax.shard_map(
        per_device, mesh=mesh, in_specs=in_specs, out_specs=out_specs, check_vma=False
    )
```
